32 devices in a mesh: grp: 2 (over y), wide: 4 (over z), tp: 4 (over x, core).
Axes of the slice: x: 2, y: 2, z: 4, core: 2. Of those that a mesh axis runs over, the one named last changes fastest.
Arguments:
- hidden: bfloat16 [24, 8192], P('grp', 'wide'), parts along dimension 0, may hold values from -6 to 6
- norm_gain: bfloat16 [8192], P('wide'), may hold values from 0.5 to 2
- query_key_value_weight: bfloat16 [8192, 10240], P('wide', 'tp'), may hold values from -0.0625 to 0.0625
- w_out: bfloat16 [8192, 8192], P('tp', 'wide'), may hold values from -0.0625 to 0.0625
- prompt_kv: bfloat16 [16, 512, 2048], P(('grp', 'wide'), None, 'tp'), parts along dimension 0, may hold values from -68 to 68
- kept_rows: int32 [16, 8, 16], P(('grp', 'wide'), 'tp'), parts along dimension 0, may hold values from 0 to 511, as said below
- owners: int32 [16], P('grp'), parts along dimension 0, may hold values from 0 to 3, as said below
- kept_len: int32 [16], P('grp'), parts along dimension 0, may hold values from 1 to 16, 96 in all
Outputs:
- state_out: bfloat16 [24, 8192], P('grp', 'wide'), parts along dimension 0
- attended: bfloat16 [24, 8192], P(('grp', 'wide'), 'tp'), parts along dimension 0
The draws below stay inside these ranges and needn't reach their ends.
There are 2 independent parts, one for each index of `grp`. The reference program is written for one: setup_inputs(seed, part) draws one part's arguments, and reference() takes and returns one part's arrays. A program takes and returns all parts, laid end to end along the dimension named above; an argument that names none is the same for every part. Nothing has to cross between parts.
Inputs may be any that keep to these rules, and one draw needn't show every extreme that they name: The 2 requests of one prefill device go to different owners; every owner receives at most 3 requests, and one owner exactly 3. `kept_rows`: each list holds distinct positions in rising order and ends with the prompt's last position.
All inputs are finite; a program needn't handle non-finite values.
Results may differ from the reference program's by a relative error of at most 0.02.
Values may be sent and summed in bfloat16 or wider, within the bound.
No kernel may reach another device: no remote copies, remote signals or barrier semaphores. Data moves between devices by JAX's collectives and lax.ppermute only.
A program may use at most 64 MiB of HBM per device.

```python
import math
import jax
import jax.numpy as jnp
import numpy as np
from jax import lax

MODEL_WIDTH = 8192
HQ = 64
KEY_HEADS = 8
HEAD_WIDTH = 128
QUERY_PER_KEY = 8
P_DEV = 2
OWN_CAP = 3
PROMPT_LENGTH = 512
KEPT_POSITIONS = 16
STEPS = 2
REQUEST_TOTAL = 8
SLOTS = 12
N_WIDE = 4


def draw_owners(key, part):
    key = jax.random.fold_in(key, 11)
    first_key, second_key, third_key = jax.random.split(key, 3)
    ordering = jax.random.permutation(first_key, N_WIDE).astype(jnp.int32)
    moved_source = jax.random.randint(second_key, (), 0, N_WIDE).astype(jnp.int32)
    moved_offset = jax.random.randint(third_key, (), 0, P_DEV).astype(jnp.int32)
    sources = jnp.arange(N_WIDE, dtype=jnp.int32)[:, None]
    offsets = jnp.arange(P_DEV, dtype=jnp.int32)[None, :]
    table = ordering[(sources + offsets) % N_WIDE]
    extra_owner = ordering[(moved_source + P_DEV) % N_WIDE]
    table = jnp.where((sources == moved_source) & (offsets == moved_offset), extra_owner, table)
    return table.reshape(REQUEST_TOTAL).astype(jnp.int32)


def draw_kept_rows(key, part):
    key = jax.random.fold_in(key, 12)
    random_row_keys = jax.random.split(key, REQUEST_TOTAL * KEY_HEADS)

    def select_rows(row_key):
        selected_rows = jax.random.permutation(row_key, PROMPT_LENGTH - 1)[:KEPT_POSITIONS - 1].astype(jnp.int32)
        last_row = jnp.full((1,), PROMPT_LENGTH - 1, jnp.int32)
        return jnp.concatenate([jnp.sort(selected_rows), last_row])
    return jax.vmap(select_rows)(random_row_keys).reshape(REQUEST_TOTAL, KEY_HEADS, KEPT_POSITIONS).astype(jnp.int32)


def draw_prompt_kv(key, part):
    key = jax.random.fold_in(key, 13)
    base_key = jax.random.fold_in(key, 0)
    every_dimension = (REQUEST_TOTAL, PROMPT_LENGTH, KEY_HEADS, 2, HEAD_WIDTH)
    value_rows = jax.random.truncated_normal(base_key, -6.0, 6.0, every_dimension, jnp.float32)
    return value_rows.reshape(REQUEST_TOTAL, PROMPT_LENGTH, KEY_HEADS * 2 * HEAD_WIDTH).astype(jnp.bfloat16)


def block_levels(rng, dims, cuts, low, top_value):
    def one(dim, blocks):
        heights = jax.random.uniform(jax.random.fold_in(jax.random.fold_in(rng, 6), dim), (blocks,), jnp.float32, low / len(cuts), top_value / len(cuts))
        return jnp.repeat(jnp.exp(heights), dims[dim] // blocks).reshape((-1,) + (1,) * (len(dims) - dim - 1))

    level = one(*cuts[0])
    for cut in cuts[1:]:
        level = level * one(*cut)
    return level


def length_profile(count, total, bound, slope):
    weights = [(1 << 20) // math.isqrt(grade ** slope) + 1 for grade in range(2, count + 1)]
    surplus, given = total - bound - (count - 1), [1] * (count - 1)
    while surplus > 0:
        candidates = [i for i in range(count - 1) if given[i] < bound]
        pool, left = sum([weights[i] for i in candidates]), surplus
        for i in candidates:
            addition = min(bound - given[i], max(1, left * weights[i] // pool), surplus)
            given[i] = given[i] + addition
            surplus = surplus - addition
    return np.array([bound] + given)


def ragged(own_key, number_of, total, limit, slope):
    if number_of == 2:
        one = jax.random.randint(own_key, (), max(1, total - limit), min(limit, total - 1) + 1)
        return jnp.stack([one, total - one])
    sizes = jnp.asarray(length_profile(number_of, total, limit, slope), jnp.int32)
    pairs = (number_of - 1) // 2
    source_of, taker = sizes[1:1 + 2 * pairs:2], sizes[2:2 + 2 * pairs:2]
    slack = jnp.minimum(source_of - 1, limit - taker)
    shifted = jax.random.randint(jax.random.fold_in(own_key, 1), (pairs,), 0, 1 << 20) % (slack + 1)
    sizes = sizes.at[1:1 + 2 * pairs:2].set(source_of - shifted).at[2:2 + 2 * pairs:2].set(taker + shifted)
    return sizes[jax.random.permutation(jax.random.fold_in(own_key, 2), number_of)]


def gaussian(key, extent, width, bound, cuts=(), kind=jnp.bfloat16):
    values = width * jax.random.normal(key, extent, jnp.float32)
    if cuts:
        values = values * block_levels(key, extent, cuts, -0.22, 0.18)
    return jnp.clip(values, -bound, bound).astype(kind)


def setup_inputs(seed: int = 0, part: int = 0) -> dict:
    key_list = jax.random.split(jax.random.key(seed), 9)
    part_splits = jax.random.split(jax.random.fold_in(key_list[8], part), 9)
    hidden = gaussian(part_splits[0], (SLOTS, MODEL_WIDTH), 1.0, 6.0, ((1, 4),))
    norm_gain = jnp.clip(jnp.exp(math.log(2.0) - 1.3862944 * jax.random.uniform(key_list[1], (MODEL_WIDTH,), jnp.float32) ** block_levels(key_list[1], (MODEL_WIDTH,), ((0, 4),), -0.2, 0.2)), 0.5, 2.0).astype(jnp.bfloat16)
    query_key_value_weight = gaussian(key_list[2], (MODEL_WIDTH, KEY_HEADS * (QUERY_PER_KEY + 2) * HEAD_WIDTH), MODEL_WIDTH ** -0.5, 0.0625, ((0, 4), (1, 4)))
    w_out = gaussian(key_list[3], (HQ * HEAD_WIDTH, MODEL_WIDTH), (HQ * HEAD_WIDTH) ** -0.5, 0.0625, ((0, 4), (1, 4)))
    prompt_kv = draw_prompt_kv(jax.random.fold_in(jax.random.fold_in(key_list[8], part), 71), part)
    kept_rows = draw_kept_rows(jax.random.fold_in(jax.random.fold_in(key_list[8], part), 71), part)
    owners = draw_owners(jax.random.fold_in(jax.random.fold_in(key_list[8], part), 71), part)
    kept_len = ragged(part_splits[7], REQUEST_TOTAL, REQUEST_TOTAL * KEPT_POSITIONS * 3 // 4, KEPT_POSITIONS, 2).astype(jnp.int32)
    return dict(hidden=hidden, norm_gain=norm_gain, query_key_value_weight=query_key_value_weight, w_out=w_out, prompt_kv=prompt_kv, kept_rows=kept_rows, owners=owners, kept_len=kept_len)


theta_base = 500000.0
eps_norm = 1e-05

def rotate(vector, position):
    half_dim = vector.shape[-1] // 2
    frequency = theta_base ** (-jnp.arange(half_dim).astype(jnp.float32) / half_dim)
    angles = position.astype(jnp.float32)[:, None, None, None] * frequency
    front_half = vector[..., :half_dim]
    back_half = vector[..., half_dim:]
    cosine = jnp.cos(angles)
    sine_part = jnp.sin(angles)
    return jnp.concatenate([front_half * cosine - back_half * sine_part, back_half * cosine + front_half * sine_part], axis=-1)

def slot_table(owners, own_cap):
    request_count = owners.shape[0]
    positions = jnp.arange(request_count, dtype=jnp.int32)
    earlier = (owners[None, :] == owners[:, None]) & (positions[None, :] < positions[:, None])
    order_rank = lax.optimization_barrier(jnp.sum(earlier.astype(jnp.int32), axis=1))
    return owners * own_cap + order_rank

def attend(queries, kept_keys, kept_values, slot_len, new_keys, new_values):
    score_scale = 1.0 / math.sqrt(queries.shape[-1])
    query_wide = queries.astype(jnp.float32)
    scores_kept = jnp.einsum('ngqd,nkgd->ngqk', query_wide, kept_keys.astype(jnp.float32)) * score_scale
    valid = jnp.arange(kept_keys.shape[1], dtype=jnp.int32)[None, :] < slot_len[:, None]
    scores_kept = jnp.where(valid[:, None, None, :], scores_kept, -1e+30)
    fresh_keys = jnp.stack(new_keys, axis=1).astype(jnp.float32)
    fresh_values = jnp.stack(new_values, axis=1).astype(jnp.float32)
    scores_new = jnp.einsum('ngqd,ntgd->ngqt', query_wide, fresh_keys) * score_scale
    highest = jnp.maximum(lax.optimization_barrier(jnp.max(scores_kept, axis=-1)), lax.optimization_barrier(jnp.max(scores_new, axis=-1)))
    weights_kept = jnp.exp(scores_kept - highest[..., None])
    weights_new = jnp.exp(scores_new - highest[..., None])
    denominator = lax.optimization_barrier(jnp.sum(weights_kept, axis=-1)) + lax.optimization_barrier(jnp.sum(weights_new, axis=-1))
    rounded_kept = weights_kept.astype(jnp.bfloat16).astype(jnp.float32)
    rounded_new = weights_new.astype(jnp.bfloat16).astype(jnp.float32)
    summed = jnp.einsum('ngqk,nkgd->ngqd', rounded_kept, kept_values.astype(jnp.float32))
    summed = summed + jnp.einsum('ngqt,ntgd->ngqd', rounded_new, fresh_values)
    result = (summed / denominator[..., None]).astype(jnp.bfloat16)
    return result.reshape(result.shape[0], -1)

def reference(hidden, norm_gain, query_key_value_weight, w_out, prompt_kv, kept_rows, owners, kept_len):
    own_cap = OWN_CAP
    slot_total = own_cap * N_WIDE
    slot_of = slot_table(owners, own_cap)
    matches = jnp.arange(slot_total, dtype=jnp.int32)[:, None] == slot_of[None, :]
    occupied = jnp.any(matches, axis=1)
    slot_req = lax.optimization_barrier(jnp.sum(jnp.where(matches, jnp.arange(REQUEST_TOTAL, dtype=jnp.int32)[None, :], 0), axis=1)).astype(jnp.int32)
    slot_len = lax.optimization_barrier(jnp.sum(jnp.where(matches, kept_len[None, :], 0), axis=1)).astype(jnp.int32)
    head_blocks = []
    for head_number in range(KEY_HEADS):
        head_block = prompt_kv[:, :, head_number * 2 * HEAD_WIDTH:(head_number + 1) * 2 * HEAD_WIDTH]
        head_blocks.append(jnp.take_along_axis(head_block, kept_rows[:, head_number, :, None].astype(jnp.int32), axis=1))
    kept_kv = jnp.stack(head_blocks, axis=2)
    cache = jnp.where(occupied[:, None, None, None], kept_kv[slot_req], jnp.zeros((), jnp.bfloat16))
    kept_keys = cache[..., :HEAD_WIDTH]
    kept_values = cache[..., HEAD_WIDTH:]
    state = hidden
    new_keys = []
    new_values = []
    attended = None
    for step_index in range(STEPS):
        state_wide = state.astype(jnp.float32)
        squares = lax.optimization_barrier(jnp.sum(state_wide * state_wide, axis=1))
        normalized_input = (state_wide * lax.rsqrt(squares / MODEL_WIDTH + eps_norm)[:, None] * norm_gain.astype(jnp.float32)).astype(jnp.bfloat16)
        projected_rows = jnp.dot(normalized_input, query_key_value_weight, preferred_element_type=jnp.float32).reshape(slot_total, KEY_HEADS, QUERY_PER_KEY + 2, HEAD_WIDTH)
        position = slot_len + step_index
        queries = rotate(projected_rows[:, :, :QUERY_PER_KEY], position).astype(jnp.bfloat16)
        key_step = rotate(projected_rows[:, :, QUERY_PER_KEY:QUERY_PER_KEY + 1], position)[:, :, 0].astype(jnp.bfloat16)
        value_step = projected_rows[:, :, QUERY_PER_KEY + 1].astype(jnp.bfloat16)
        new_keys.append(key_step)
        new_values.append(value_step)
        attended = attend(queries, kept_keys, kept_values, slot_len, new_keys, new_values)
        state = (state_wide + jnp.dot(attended, w_out, preferred_element_type=jnp.float32)).astype(jnp.bfloat16)
    return (state, attended)
```

```python
import math

import jax
import jax.numpy as jnp
from jax import lax
from jax.sharding import PartitionSpec as P

HEAD_WIDTH = 128
QUERY_PER_KEY = 8
STEPS = 2
DIRECT_LIMIT = 8

theta_base = 500000.0
eps_norm = 1e-05


def exchange_sum(partial, axis):
    count = lax.axis_size(axis)
    if count > DIRECT_LIMIT:
        return lax.psum(partial.astype(jnp.float32), axis)
    terms = [partial.astype(jnp.float32)]
    for offset in range(1, count):
        pairs = [(i, i ^ offset) for i in range(count)]
        terms.append(lax.ppermute(partial, axis, pairs).astype(jnp.float32))
    while len(terms) > 1:
        terms = [terms[i] + terms[i + 1] for i in range(0, len(terms), 2)]
    return terms[0]


def exchange_gather(block, axis):
    count = lax.axis_size(axis)
    if count > DIRECT_LIMIT:
        return lax.all_gather(block, axis, axis=0, tiled=True)
    blocks = [block]
    for offset in range(1, count):
        pairs = [(i, i ^ offset) for i in range(count)]
        blocks.append(lax.ppermute(block, axis, pairs))
    return blocks


def rotate(vector, cosine, sine):
    half = vector.shape[-1] // 2
    front, back = vector[..., :half], vector[..., half:]
    return jnp.concatenate([front * cosine - back * sine, back * cosine + front * sine], axis=-1)


def shards(
    hidden, norm_gain, query_key_value_weight, w_out, prompt_kv, kept_rows, owners, kept_len
):
    wide_count = lax.axis_size("wide")
    me = lax.axis_index("wide")
    slots = hidden.shape[0]
    own_cap = slots // wide_count
    model_width = hidden.shape[1] * wide_count
    requests_dev, heads = kept_rows.shape[0], kept_rows.shape[1]
    kept_positions = kept_rows.shape[2]
    requests = owners.shape[0]

    ids = jnp.arange(requests, dtype=jnp.int32)
    earlier = (owners[None, :] == owners[:, None]) & (ids[None, :] < ids[:, None])
    slot_of = owners * own_cap + jnp.sum(earlier.astype(jnp.int32), axis=1)
    matches = jnp.arange(slots, dtype=jnp.int32)[:, None] == slot_of[None, :]
    slot_len = jnp.sum(jnp.where(matches, kept_len[None, :], 0), axis=1)

    length = prompt_kv.shape[1]
    pick = (
        kept_rows[..., None] == jnp.arange(length, dtype=jnp.int32)
    ).astype(jnp.bfloat16)
    kept = jnp.einsum(
        "rgkp,rpgc->rgkc",
        pick,
        prompt_kv.reshape(requests_dev, length, heads, 2 * HEAD_WIDTH),
        preferred_element_type=jnp.float32,
    ).astype(jnp.bfloat16)
    blocks = exchange_gather(kept, "wide")
    if isinstance(blocks, list):
        cache = 0.0
        for offset, block in enumerate(blocks):
            source = me ^ offset
            columns = lax.dynamic_slice_in_dim(matches, source * requests_dev, requests_dev, axis=1)
            cache = cache + jnp.einsum(
                "sr,rgkc->sgkc",
                columns.astype(jnp.bfloat16),
                block,
                preferred_element_type=jnp.float32,
            )
        cache = cache.astype(jnp.bfloat16)
    else:
        cache = jnp.einsum(
            "sr,rgkc->sgkc",
            matches.astype(jnp.bfloat16),
            blocks,
            preferred_element_type=jnp.float32,
        ).astype(jnp.bfloat16)
    keys, values = cache[..., :HEAD_WIDTH], cache[..., HEAD_WIDTH:]
    valid = jnp.arange(kept_positions, dtype=jnp.int32)[None, :] < slot_len[:, None]
    score_scale = 1.0 / math.sqrt(HEAD_WIDTH)

    half = HEAD_WIDTH // 2
    frequency = theta_base ** (-jnp.arange(half).astype(jnp.float32) / half)
    gain = norm_gain.astype(jnp.float32)
    state = hidden
    new_keys, new_values = [], []
    attended = None
    for step in range(STEPS):
        state_wide = state.astype(jnp.float32)
        squares = jnp.sum(state_wide * state_wide, axis=1)
        high = squares.astype(jnp.bfloat16)
        low = (squares - high.astype(jnp.float32)).astype(jnp.bfloat16)
        product = jnp.dot(
            (state_wide * gain).astype(jnp.bfloat16),
            query_key_value_weight,
            preferred_element_type=jnp.float32,
        ).astype(jnp.bfloat16)
        tail = jnp.concatenate(
            [jnp.broadcast_to(high[:, None], (slots, 64)), jnp.broadcast_to(low[:, None], (slots, 64))],
            axis=1,
        )
        total = exchange_sum(jnp.concatenate([product, tail], axis=1), "wide")
        squares = total[:, -128] + total[:, -1]
        scale = lax.rsqrt(squares / model_width + eps_norm)
        proj = (total[:, :-128] * scale[:, None]).reshape(slots, heads, QUERY_PER_KEY + 2, HEAD_WIDTH)
        angles = (slot_len + step).astype(jnp.float32)[:, None, None, None] * frequency
        turned = rotate(proj[:, :, : QUERY_PER_KEY + 1], jnp.cos(angles), jnp.sin(angles)).astype(
            jnp.bfloat16
        )
        queries = turned[:, :, :QUERY_PER_KEY]
        new_keys.append(turned[:, :, QUERY_PER_KEY])
        new_values.append(proj[:, :, QUERY_PER_KEY + 1].astype(jnp.bfloat16))
        fresh_keys, fresh_values = jnp.stack(new_keys, axis=2), jnp.stack(new_values, axis=2)
        all_keys = jnp.concatenate([keys, fresh_keys], axis=2)
        all_values = jnp.concatenate([values, fresh_values], axis=2)
        scores = (
            jnp.einsum("ngqd,ngkd->ngqk", queries, all_keys, preferred_element_type=jnp.float32)
            * score_scale
        )
        live = jnp.concatenate([valid, jnp.ones((slots, step + 1), bool)], axis=1)
        scores = jnp.where(live[:, None, None, :], scores, -1e30)
        weights = jnp.exp(scores - jnp.max(scores, axis=-1, keepdims=True))
        denominator = jnp.sum(weights, axis=-1, keepdims=True)
        summed = jnp.einsum(
            "ngqk,ngkd->ngqd",
            weights.astype(jnp.bfloat16),
            all_values,
            preferred_element_type=jnp.float32,
        )
        attended = (summed / denominator).astype(jnp.bfloat16).reshape(slots, -1)
        partial_rows = jnp.dot(attended, w_out, preferred_element_type=jnp.float32)
        state = (state_wide + exchange_sum(partial_rows.astype(jnp.bfloat16), "tp")).astype(
            jnp.bfloat16
        )
    return state, lax.dynamic_slice_in_dim(attended, me * own_cap, own_cap, axis=0)


def solution(mesh):
    in_specs = (
        P("grp", "wide"),
        P("wide"),
        P("wide", "tp"),
        P("tp", "wide"),
        P(("grp", "wide"), None, "tp"),
        P(("grp", "wide"), "tp", None),
        P("grp"),
        P("grp"),
    )
    out_specs = (P("grp", "wide"), P(("grp", "wide"), "tp"))
    return jax.shard_map(shards, mesh=mesh, in_specs=in_specs, out_specs=out_specs, check_vma=False)
```

```python
import math

import jax
import jax.numpy as jnp
from jax import lax
from jax.sharding import PartitionSpec as P

HEAD_WIDTH = 128
QUERY_PER_KEY = 8
STEPS = 2
DIRECT_LIMIT = 8

theta_base = 500000.0
eps_norm = 1e-05


def exchange_gather(block, axis):
    count = lax.axis_size(axis)
    if count > DIRECT_LIMIT:
        return lax.all_gather(block, axis, axis=0)
    copies = jnp.broadcast_to(block[None], (count,) + block.shape)
    return lax.all_to_all(copies, axis, split_axis=0, concat_axis=0)


def exchange_sum(partial, axis):
    if lax.axis_size(axis) > DIRECT_LIMIT:
        return lax.psum(partial.astype(jnp.float32), axis)
    return jnp.sum(exchange_gather(partial, axis).astype(jnp.float32), axis=0)


def rotate(vector, cosine, sine):
    half = vector.shape[-1] // 2
    front, back = vector[..., :half], vector[..., half:]
    return jnp.concatenate([front * cosine - back * sine, back * cosine + front * sine], axis=-1)


def shards(
    hidden, norm_gain, query_key_value_weight, w_out, prompt_kv, kept_rows, owners, kept_len
):
    wide_count = lax.axis_size("wide")
    me = lax.axis_index("wide")
    slots = hidden.shape[0]
    own_cap = slots // wide_count
    model_width = hidden.shape[1] * wide_count
    requests_dev, heads = kept_rows.shape[0], kept_rows.shape[1]
    kept_positions = kept_rows.shape[2]
    requests = owners.shape[0]

    ids = jnp.arange(requests, dtype=jnp.int32)
    earlier = (owners[None, :] == owners[:, None]) & (ids[None, :] < ids[:, None])
    slot_of = owners * own_cap + jnp.sum(earlier.astype(jnp.int32), axis=1)
    matches = jnp.arange(slots, dtype=jnp.int32)[:, None] == slot_of[None, :]
    slot_len = jnp.sum(jnp.where(matches, kept_len[None, :], 0), axis=1)

    length = prompt_kv.shape[1]
    pick = (
        kept_rows[..., None] == jnp.arange(length, dtype=jnp.int32)
    ).astype(jnp.bfloat16)
    kept = jnp.einsum(
        "rgkp,rpgc->rgkc",
        pick,
        prompt_kv.reshape(requests_dev, length, heads, 2 * HEAD_WIDTH),
        preferred_element_type=jnp.float32,
    ).astype(jnp.bfloat16)
    blocks = exchange_gather(kept, "wide")
    blocks = blocks.reshape((requests,) + kept.shape[1:])
    cache = jnp.einsum(
        "sr,rgkc->sgkc",
        matches.astype(jnp.bfloat16),
        blocks,
        preferred_element_type=jnp.float32,
    ).astype(jnp.bfloat16)
    keys, values = cache[..., :HEAD_WIDTH], cache[..., HEAD_WIDTH:]
    valid = jnp.arange(kept_positions, dtype=jnp.int32)[None, :] < slot_len[:, None]
    score_scale = 1.0 / math.sqrt(HEAD_WIDTH)

    half = HEAD_WIDTH // 2
    frequency = theta_base ** (-jnp.arange(half).astype(jnp.float32) / half)
    gain = norm_gain.astype(jnp.float32)
    state = hidden
    new_keys, new_values = [], []
    attended = None
    for step in range(STEPS):
        state_wide = state.astype(jnp.float32)
        squares = jnp.sum(state_wide * state_wide, axis=1)
        high = squares.astype(jnp.bfloat16)
        low = (squares - high.astype(jnp.float32)).astype(jnp.bfloat16)
        product = jnp.dot(
            (state_wide * gain).astype(jnp.bfloat16),
            query_key_value_weight,
            preferred_element_type=jnp.float32,
        ).astype(jnp.bfloat16)
        tail = jnp.concatenate(
            [jnp.broadcast_to(high[:, None], (slots, 64)), jnp.broadcast_to(low[:, None], (slots, 64))],
            axis=1,
        )
        total = exchange_sum(jnp.concatenate([product, tail], axis=1), "wide")
        squares = total[:, -128] + total[:, -1]
        scale = lax.rsqrt(squares / model_width + eps_norm)
        proj = (total[:, :-128] * scale[:, None]).reshape(slots, heads, QUERY_PER_KEY + 2, HEAD_WIDTH)
        angles = (slot_len + step).astype(jnp.float32)[:, None, None, None] * frequency
        turned = rotate(proj[:, :, : QUERY_PER_KEY + 1], jnp.cos(angles), jnp.sin(angles)).astype(
            jnp.bfloat16
        )
        queries = turned[:, :, :QUERY_PER_KEY]
        new_keys.append(turned[:, :, QUERY_PER_KEY])
        new_values.append(proj[:, :, QUERY_PER_KEY + 1].astype(jnp.bfloat16))
        fresh_keys, fresh_values = jnp.stack(new_keys, axis=2), jnp.stack(new_values, axis=2)
        all_keys = jnp.concatenate([keys, fresh_keys], axis=2)
        all_values = jnp.concatenate([values, fresh_values], axis=2)
        scores = (
            jnp.einsum("ngqd,ngkd->ngqk", queries, all_keys, preferred_element_type=jnp.float32)
            * score_scale
        )
        live = jnp.concatenate([valid, jnp.ones((slots, step + 1), bool)], axis=1)
        scores = jnp.where(live[:, None, None, :], scores, -1e30)
        weights = jnp.exp(scores - jnp.max(scores, axis=-1, keepdims=True))
        denominator = jnp.sum(weights, axis=-1, keepdims=True)
        summed = jnp.einsum(
            "ngqk,ngkd->ngqd",
            weights.astype(jnp.bfloat16),
            all_values,
            preferred_element_type=jnp.float32,
        )
        attended = (summed / denominator).astype(jnp.bfloat16).reshape(slots, -1)
        partial_rows = jnp.dot(attended, w_out, preferred_element_type=jnp.float32)
        state = (state_wide + exchange_sum(partial_rows.astype(jnp.bfloat16), "tp")).astype(
            jnp.bfloat16
        )
    return state, lax.dynamic_slice_in_dim(attended, me * own_cap, own_cap, axis=0)


def solution(mesh):
    in_specs = (
        P("grp", "wide"),
        P("wide"),
        P("wide", "tp"),
        P("tp", "wide"),
        P(("grp", "wide"), None, "tp"),
        P(("grp", "wide"), "tp", None),
        P("grp"),
        P("grp"),
    )
    out_specs = (P("grp", "wide"), P(("grp", "wide"), "tp"))
    return jax.shard_map(shards, mesh=mesh, in_specs=in_specs, out_specs=out_specs, check_vma=False)
```
